512 devices in a mesh: dp: 64 (over x_hi, z, core), space: 8 (over x_lo, y).
Axes of the slice: x: 4 (x_hi: 2, x_lo: 2; x = x_hi * 2 + x_lo), y: 4, z: 16, core: 2. Of those that a mesh axis runs over, the one named last changes fastest.
Arguments:
- features: bfloat16 [131072, 128], P(('dp', 'space')), may hold values from -6 to 6
- teacher: bfloat16 [131072, 256], P(('dp', 'space')), may hold values from -6 to 6
- weight: bfloat16 [3456, 256], replicated, may hold values from -0.109375 to 0.109375
- neighbours: int32 [131072, 27], P(('dp', 'space')), may hold values from -1 to 383, as said below
- counts: int32 [512], replicated, may hold values from 128 to 256, as said below
Outputs:
- grad_input: bfloat16 [131072, 128], P(('dp', 'space'))
- grad_weight: float32 [3456, 256], P('dp')
- loss: float32 [], replicated
The draws below stay inside these ranges and needn't reach their ends.
Inputs may be any that keep to these rules, and one draw needn't show every extreme that they name: `neighbours`: window positions below 64 lie on the device one lower along space, positions 320 and up on the device one higher, and every named slot is valid and of the same scene. Offset 13 of a valid site names the site itself; padding slots have -1 everywhere. `counts`: some device has all 256 slots valid.
All inputs are finite; a program needn't handle non-finite values.
Results may differ from the reference program's by a relative error of at most 0.0075.
Values may be sent and summed in bfloat16 or wider, within the bound.
A program may use at most 64 MiB of HBM per device.

```python
import jax
import jax.numpy as jnp
from jax import lax

C_IN = 128
C_OUT = 256
K = 27
S_DEV = 256
EDGE = 64
SITES = 131072
N_DP = 64
N_SPACE = 8


def device_counts(key):
    n_dev = SITES // S_DEV
    key_a, key_b = jax.random.split(key)
    drawn = jax.random.randint(key_a, (n_dev,), S_DEV // 2, S_DEV + 1)
    full_dev = jax.random.randint(key_b, (), 0, n_dev)
    return jnp.where(jnp.arange(n_dev) == full_dev, S_DEV, drawn).astype(jnp.int32)


def draw_counts(key, part):
    return device_counts(key)


def draw_neighbours(key, part):
    cnts = device_counts(key)
    key = jax.random.fold_in(key, 7)
    n_dev = SITES // S_DEV
    keys = jax.random.split(key, 4)
    shape = (n_dev, S_DEV, K)
    dev = jnp.arange(n_dev)[:, None, None]
    slot = jnp.arange(S_DEV)[None, :, None]
    offs = jnp.arange(K)[None, None, :]
    limit = cnts[:, None, None]
    pick = jax.random.randint(keys[0], shape, 0, 2 ** 30) % limit
    local = jnp.where(pick < limit - EDGE, pick, S_DEV - EDGE + pick - (limit - EDGE))
    own_src = dev * S_DEV + local
    lower_src = (dev - 1) * S_DEV + S_DEV - EDGE + jax.random.randint(keys[1], shape, 0, EDGE)
    upper_src = (dev + 1) * S_DEV + jax.random.randint(keys[2], shape, 0, EDGE)
    place = dev % N_SPACE
    use_lower = (slot < EDGE) & (offs < 13) & (place > 0)
    use_upper = (slot >= S_DEV - EDGE) & (offs > 13) & (place < N_SPACE - 1)
    source = jnp.where(use_lower, lower_src, jnp.where(use_upper, upper_src, own_src))
    exists = jax.random.randint(keys[3], shape, 0, 10) < 7
    itself = dev * S_DEV + slot + 0 * offs
    source = jnp.where(offs == 13, itself, jnp.where(exists, source, -1))
    forced = (dev == 0) & (slot == S_DEV - 1) & (offs == K - 1)
    source = jnp.where(forced, S_DEV + EDGE - 1, source)
    valid = (slot < limit - EDGE) | (slot >= S_DEV - EDGE)
    source = jnp.where(valid, source, -1)
    window = jnp.where(source < 0, -1, source - dev * S_DEV + EDGE)
    return window.reshape(SITES, K).astype(jnp.int32)


def shard_levels(rng, shape, shards, least, top_value):
    loudness, own = 1.0, jax.random.fold_in(rng, 6)
    for axis_at, parts in shards:
        steps = jnp.exp(jax.random.uniform(jax.random.fold_in(own, axis_at), (parts,), jnp.float32, least / len(shards), top_value / len(shards)))
        loudness = loudness * jnp.repeat(steps, shape[axis_at] // parts).reshape([-1 if axis == axis_at else 1 for axis in range(len(shape))])
    return loudness


def normal_values(key, extent, scale, bound, cuts=(), kind=jnp.bfloat16):
    level = shard_levels(key, extent, cuts, -0.22, 0.18) if cuts else 1.0
    values = jax.random.normal(key, extent, jnp.float32) * scale * level
    return jnp.minimum(jnp.maximum(values, -bound), bound).astype(kind)


def setup_inputs(seed: int = 0) -> dict:
    key_of = jax.random.split(jax.random.key(seed), 6)
    return {
        "features": normal_values(key_of[0], (SITES, C_IN), 1.0, 6.0, ((0, 512),)),
        "teacher": normal_values(key_of[1], (SITES, C_OUT), 1.0, 6.0, ((0, 512),)),
        "weight": normal_values(key_of[2], (K * C_IN, C_OUT), (K * C_IN) ** -0.5, 0.109375),
        "neighbours": draw_neighbours(jax.random.fold_in(key_of[5], 71), 0),
        "counts": draw_counts(jax.random.fold_in(key_of[5], 71), 0),
    }


def reference(features, teacher, weight, neighbours, counts):
    per = S_DEV * N_SPACE
    scene_feats = features.reshape(N_DP, per, C_IN)
    scene_teach = teacher.reshape(N_DP, per, C_OUT)
    scene_nbrs = neighbours.reshape(N_DP, per, K)
    scene_counts = counts.reshape(N_DP, N_SPACE)
    slots = jnp.arange(per, dtype=jnp.int32) % S_DEV
    base = (jnp.arange(per, dtype=jnp.int32) // S_DEV) * S_DEV

    def one_scene(carry, items):
        grad_acc, square_acc = carry
        feats, teach, nbrs, cnts = items
        index = jnp.where(nbrs < 0, per, nbrs + base[:, None] - EDGE).astype(jnp.int32)
        padded = jnp.concatenate([feats, jnp.zeros((1, C_IN), jnp.bfloat16)], axis=0)
        gathered = jnp.take(padded, index, axis=0).reshape(per, K * C_IN)
        z_out = jnp.dot(gathered, weight, preferred_element_type=jnp.float32)
        limit = jnp.repeat(cnts, S_DEV)
        valid = (slots < limit - EDGE) | (slots >= S_DEV - EDGE)
        diff = jnp.where(valid[:, None], z_out - teach.astype(jnp.float32), jnp.float32(0.0))
        squares = jnp.sum(diff * diff)
        grad_z = (diff / C_OUT).astype(jnp.bfloat16)
        grad_w = lax.dot_general(gathered, grad_z, (((0,), (0,)), ((), ())), preferred_element_type=jnp.float32)
        grad_g = jnp.dot(grad_z, weight.T, preferred_element_type=jnp.float32)
        spread = jax.ops.segment_sum(grad_g.reshape(per * K, C_IN), index.reshape(-1), num_segments=per + 1)
        grad_x = spread[:per].astype(jnp.bfloat16)
        return (grad_acc + grad_w, square_acc + squares), grad_x

    init = (jnp.zeros((K * C_IN, C_OUT), jnp.float32), jnp.float32(0.0))
    (grad_weight, total_sq), grad_x = lax.scan(one_scene, init, (scene_feats, scene_teach, scene_nbrs, scene_counts))
    loss = 0.5 * total_sq / (C_OUT * jnp.sum(counts).astype(jnp.float32))
    return grad_x.reshape(SITES, C_IN), grad_weight, loss
```

```python
import functools

import jax
import jax.numpy as jnp
from jax import lax
from jax.experimental import pallas as pl
from jax.experimental.pallas import tpu as pltpu
from jax.sharding import PartitionSpec as P

F32 = jnp.float32
BF16 = jnp.bfloat16
MESH = pl.DeviceIdType.MESH
ORDERS = (("xp", "xq", "yp", "yq"), ("xq", "xp", "yq", "yp"), ("yp", "yq", "xp", "xq"), ("yq", "yp", "xq", "xp"))
NT = (((1,), (1,)), ((), ()))


def dot(a, b):
    return jnp.dot(a, b, preferred_element_type=F32)


def dot_nt(a, b):
    return lax.dot_general(a, b, NT, preferred_element_type=F32)


def body(n_dp, n_space, comm, feats, teacher, weight, nbrs, counts,
         out_x, out_w, out_loss,
         win, nbr_v, teach_v, w_v, w_t, hot, g_t, gw, part, rc, s0, r1, s1, r2, s2, r3, s3, r4, s4,
         rz, ag, gsend, grecv, lsum, lrecv,
         lsem, halo_s, halo_r, core_s, core_r, step_s, step_r, z_s, z_r, ag_s, ag_r, gh_s, gh_r, loss_s, loss_r):
    sites, chans = feats.shape
    outs = teacher.shape[1]
    offsets = nbrs.shape[0]
    edge = sites // 4
    slots = sites + 2 * edge
    nz = n_dp // 4
    z4 = nz // 4
    rows = offsets * chans // n_dp

    dp, sp = lax.axis_index("dp"), lax.axis_index("space")
    core = dp % 2
    z = (dp // 2) % nz
    xh = dp // (2 * nz)
    xl, y = sp // 4, sp % 4
    bit = {"xp": (xl + xh) % 2, "xq": xh, "yp": (y % 2 + y // 2) % 2, "yq": y // 2}
    x = 2 * xh + xl
    xq = (x + 2 * xl + 3) % 4
    peer = {
        "xp": (dp, (1 - xl) * 4 + y),
        "xq": (dp + (xq // 2 - xh) * 2 * nz, (xq % 2) * 4 + y),
        "yp": (dp, xl * 4 + y + 1 - 2 * (y % 2)),
        "yq": (dp, xl * 4 + (y + 2 * (y % 2) + 3) % 4),
        "core": (dp + 1 - 2 * core, sp),
    }

    def z_peer(zz):
        return (xh * 2 * nz + zz * 2 + core, sp)

    def sp_peer(step):
        return (dp, (sp + step) % n_space)

    def piece_of(space):
        l, w = space // 4, space % 4
        return ((l + xh) % 2) * 4 + ((w % 2 + w // 2) % 2) * 2 + w // 2

    def remote(src, dst, send, recv, device):
        return pltpu.make_async_remote_copy(
            src_ref=src, dst_ref=dst, send_sem=send, recv_sem=recv, device_id=device, device_id_type=MESH)

    sent = []

    def start(copy):
        if comm:
            copy.start()
            sent.append(copy)

    def got(copy):
        if comm:
            copy.wait_recv()

    own_in = pltpu.make_async_copy(feats, win.at[pl.ds(edge, sites)], lsem.at[0])
    nbr_in = pltpu.make_async_copy(nbrs, nbr_v, lsem.at[1])
    w_in = pltpu.make_async_copy(weight, w_v, lsem.at[2])
    t_in = pltpu.make_async_copy(teacher, teach_v, lsem.at[3])
    nbr_in.start()
    own_in.start()
    w_in.start()
    t_in.start()
    if comm:
        barrier = pltpu.get_barrier_semaphore()
        partners = [sp_peer(i) for i in range(1, n_space)] + [peer["xq"], peer["core"]]
        for device in partners:
            pl.semaphore_signal(barrier, inc=1, device_id=device, device_id_type=MESH)

        @pl.loop(1, nz)
        def _(i):
            pl.semaphore_signal(barrier, inc=1, device_id=z_peer((z + i) % nz), device_id_type=MESH)

        pl.semaphore_wait(barrier, len(partners) + nz - 1)

    halo_up = remote(feats.at[pl.ds(sites - edge, edge)], win.at[pl.ds(0, edge)], halo_s.at[0], halo_r.at[0], sp_peer(1))
    halo_dn = remote(feats.at[pl.ds(0, edge)], win.at[pl.ds(edge + sites, edge)], halo_s.at[1], halo_r.at[1],
                     sp_peer(n_space - 1))
    start(halo_up)
    start(halo_dn)

    nbr_in.wait()
    nbr_t = nbr_v[...]
    slot = lax.broadcasted_iota(jnp.int32, (slots, sites), 0)
    for k in range(offsets):
        hot[k] = (slot == nbr_t[k:k + 1, :]).astype(F32).astype(BF16)

    eye = (lax.broadcasted_iota(jnp.int32, (outs, outs), 0) == lax.broadcasted_iota(jnp.int32, (outs, outs), 1))
    eye = eye.astype(F32).astype(BF16)
    w_in.wait()
    for k in range(offsets):
        w_t[:, k * chans:(k + 1) * chans] = dot_nt(eye, w_v[k * chans:(k + 1) * chans, :]).astype(BF16)
    t_in.wait()
    teach_t = dot_nt(eye, teach_v[...])

    count = counts[...]
    flat = lax.broadcasted_iota(jnp.int32, count.shape, 0) * count.shape[1] + lax.broadcasted_iota(
        jnp.int32, count.shape, 1)
    limit = jnp.sum(jnp.where(flat == dp * n_space + sp, count, 0))
    total_count = jnp.sum(count)

    own_in.wait()
    got(halo_up)
    got(halo_dn)
    win_t = dot_nt(eye[:chans, :chans], win[...]).astype(BF16)
    for k in range(offsets):
        g_t[k * chans:(k + 1) * chans, :] = dot(win_t, hot[k]).astype(BF16)
    z_t = dot(w_t[...], g_t[...])
    at = lax.broadcasted_iota(jnp.int32, (outs, sites), 1)
    diff = jnp.where((at < limit - edge) | (at >= sites - edge), z_t - teach_t, F32(0.0))
    dz_t = (diff / outs).astype(BF16)
    square = jnp.sum((diff * diff).reshape(outs // 8, 8, sites), axis=0)
    lsum[0] = square[:, :128] + square[:, 128:]

    chain = ["core", "xp", "xq", "yp", "yq"]
    hop = 1
    while hop < nz:
        chain.append(hop)
        hop *= 2

    def loss_copy(i):
        if i < 5:
            device = peer[chain[i]]
        else:
            device = z_peer(z + chain[i] - 2 * chain[i] * ((z // chain[i]) % 2))
        return remote(lsum.at[i], lrecv.at[i], loss_s.at[i], loss_r.at[i], device)

    loss_copies = [loss_copy(i) for i in range(len(chain))]

    def loss_step(i):
        if i >= len(chain):
            return
        got(loss_copies[i])
        lsum[i + 1] = lsum[i] + lrecv[i]
        if i + 1 < len(chain):
            start(loss_copies[i + 1])

    start(loss_copies[0])

    held = [s0, s1, s2, s3, s4]
    come = [rc, r1, r2, r3, r4]
    core_copies = [remote(part.at[1 - core, s], rc.at[s], core_s.at[s], core_r.at[s], peer["core"]) for s in range(4)]
    step_copies = []
    for i in range(4):
        half = 8 >> i
        step_copies.append([
            remote(held[i].at[s, pl.ds((1 - bit[ORDERS[s][i]]) * half, half)], come[i + 1].at[s],
                   step_s.at[i, s], step_r.at[i, s], peer[ORDERS[s][i]]) for s in range(4)])

    def after_core(s):
        got(core_copies[s])

        @pl.loop(0, 16)
        def _(i):
            s0[s, i] = (part[core, s, i].astype(F32) + rc[s, i].astype(F32)).astype(BF16)
        start(step_copies[0][s])

    def after_step(i, s):
        got(step_copies[i][s])
        half = 8 >> i
        mine = bit[ORDERS[s][i]] * half
        for q in range(half):
            held[i + 1][s, q] = (held[i][s, mine + q].astype(F32) + come[i + 1][s, q].astype(F32)).astype(BF16)
        if i < 3:
            start(step_copies[i + 1][s])
        elif comm:
            for j in range(z4):
                to = s * z4 + j
                back = (to - z + nz) % nz

                @pl.when(back != 0)
                def _():
                    remote(s4.at[s, 0, j], rz.at[back], z_s.at[back], z_r.at[back], z_peer(to)).start()

    block = 2 * z4 * rows
    gw[:, block:, :] = jnp.zeros((2, gw.shape[1] - block, outs), F32)
    for s in range(4):
        dims = ORDERS[s]
        for h in range(2):
            base = (h * 4 + s) * block
            gw[h, :block, :] = dot_nt(g_t[base:base + block, :], dz_t)
            for j in range(z4):
                for c in range(2):
                    frame = gw[h, (j * 2 + c) * rows:(j * 2 + c) * rows + 64, :].astype(BF16)
                    for p in range(8):
                        val = {"xp": p // 4, "xq": h, "yp": (p // 2) % 2, "yq": p % 2}
                        index = 0
                        for d in dims:
                            index = index * 2 + val[d]
                        q = p % 4
                        part[c, s, index, j] = frame[16 * q:16 * q + 16, 128 * (p // 4):128 * (p // 4) + 128]
        start(core_copies[s])
        if s > 0:
            after_core(s - 1)
            loss_step(s - 1)
    after_core(3)

    def spread_part(first, last, acc):
        for k in range(first, last):
            d_t = dot(w_v[k * chans:(k + 1) * chans, :], dz_t).astype(BF16)
            acc = acc + dot_nt(d_t, hot[k])
        return acc

    spread = spread_part(0, offsets, jnp.zeros((chans, slots), F32))
    own = jnp.transpose(spread)
    gsend[0] = own[:edge].astype(BF16)
    gsend[1] = own[edge + sites:].astype(BF16)
    gh_dn = remote(gsend.at[0], grecv.at[0], gh_s.at[0], gh_r.at[0], sp_peer(n_space - 1))
    gh_up = remote(gsend.at[1], grecv.at[1], gh_s.at[1], gh_r.at[1], sp_peer(1))
    start(gh_dn)
    start(gh_up)
    loss_step(3)

    for s in range(4):
        after_step(0, s)
    loss_step(4)
    for s in range(4):
        after_step(1, s)
    loss_step(5)

    got(gh_dn)
    got(gh_up)
    out_x[edge:sites - edge, :] = own[2 * edge:sites].astype(BF16)
    out_x[:edge, :] = (own[edge:2 * edge] + grecv[1].astype(F32)).astype(BF16)
    out_x[sites - edge:, :] = (own[sites:sites + edge] + grecv[0].astype(F32)).astype(BF16)

    for s in range(4):
        after_step(2, s)
    loss_step(6)
    for s in range(4):
        after_step(3, s)
    loss_step(7)
    loss_step(8)

    total = s4[z // z4, 0, z % z4].astype(F32)
    if comm:
        for t in range(1, nz):
            incoming = remote(rz.at[t], rz.at[t], z_s.at[t], z_r.at[t], z_peer(z))
            incoming.wait_recv()
            total = total + rz[t].astype(F32)
    mine = piece_of(sp)
    ag[mine] = total
    ag_copies = []
    for u in range(1, n_space):
        copy = remote(ag.at[mine], ag.at[mine], ag_s.at[u], ag_r.at[u], sp_peer(u))
        start(copy)
    loss_total = jnp.sum(lsum[len(chain)])
    out_loss[0, 0] = 0.5 * loss_total / (outs * total_count.astype(F32))
    if comm:
        for u in range(1, n_space):
            source = piece_of((sp - u + n_space) % n_space)
            remote(ag.at[source], ag.at[source], ag_s.at[u], ag_r.at[u], sp_peer(u)).wait_recv()
    for p in range(8):
        q, h = p % 4, p // 4
        keep = min(16, rows - 16 * q)
        out_w[16 * q:16 * q + keep, 128 * h:128 * h + 128] = ag[p][:keep]
    for copy in sent:
        copy.wait_send()
    if comm:
        for t in range(1, nz):
            remote(rz.at[t], rz.at[t], z_s.at[t], z_r.at[t], z_peer(z)).wait_send()


def shards(n_dp, n_space, comm, features, teacher, weight, neighbours, counts):
    sites, chans = features.shape
    outs = teacher.shape[1]
    offsets = neighbours.shape[1]
    edge = sites // 4
    slots = sites + 2 * edge
    nz = n_dp // 4
    z4 = nz // 4
    rows = offsets * chans // n_dp
    assert 48 < rows <= 64 and n_space == 8 and outs == 256 and chans == 128
    n_loss = 5 + (nz - 1).bit_length()
    tile = (16, 128)
    levels = []
    for i in range(1, 5):
        levels += [pltpu.VMEM((4, 16 >> i, z4) + tile, BF16)] * 2
    dma = pltpu.SemaphoreType.DMA
    grad_x, grad_w, loss = pl.pallas_call(
        functools.partial(body, n_dp, n_space, comm),
        out_shape=(
            jax.ShapeDtypeStruct((sites, chans), BF16),
            jax.ShapeDtypeStruct((rows, outs), F32),
            jax.ShapeDtypeStruct((1, 1), F32),
        ),
        in_specs=[pl.BlockSpec(memory_space=pl.ANY)] * 4 + [pl.BlockSpec(memory_space=pltpu.VMEM)],
        out_specs=(
            pl.BlockSpec(memory_space=pltpu.VMEM),
            pl.BlockSpec(memory_space=pltpu.VMEM),
            pl.BlockSpec(memory_space=pltpu.SMEM),
        ),
        scratch_shapes=[
            pltpu.VMEM((slots, chans), BF16),
            pltpu.VMEM((offsets, sites), jnp.int32),
            pltpu.VMEM((sites, outs), BF16),
            pltpu.VMEM((offsets * chans, outs), BF16),
            pltpu.VMEM((outs, offsets * chans), BF16),
            pltpu.VMEM((offsets, slots, sites), BF16),
            pltpu.VMEM((offsets * chans, sites), BF16),
            pltpu.VMEM((2, 2 * z4 * rows + 16, outs), F32),
            pltpu.VMEM((2, 4, 16, z4) + tile, BF16),
            pltpu.VMEM((4, 16, z4) + tile, BF16),
            pltpu.VMEM((4, 16, z4) + tile, BF16),
        ] + levels + [
            pltpu.VMEM((nz,) + tile, BF16),
            pltpu.VMEM((8,) + tile, F32),
            pltpu.VMEM((2, edge, chans), BF16),
            pltpu.VMEM((2, edge, chans), BF16),
            pltpu.VMEM((n_loss + 1, 8, 128), F32),
            pltpu.VMEM((n_loss, 8, 128), F32),
            dma((4,)), dma((2,)), dma((2,)), dma((4,)), dma((4,)), dma((4, 4)), dma((4, 4)),
            dma((nz,)), dma((nz,)), dma((n_space,)), dma((n_space,)), dma((2,)), dma((2,)),
            dma((n_loss,)), dma((n_loss,)),
        ],
        compiler_params=pltpu.CompilerParams(
            vmem_limit_bytes=48 * 1024 * 1024,
            **(dict(collective_id=0, has_side_effects=True) if comm else {})),
    )(features, teacher, weight, neighbours.T, counts.reshape(-1, 128))
    return grad_x, grad_w, loss.reshape(())


def solution(mesh, comm=True):
    placed = (
        P(("dp", "space"), None),
        P(("dp", "space"), None),
        P(),
        P(("dp", "space"), None),
        P(),
    )
    return jax.shard_map(
        functools.partial(shards, mesh.shape["dp"], mesh.shape["space"], comm),
        mesh=mesh,
        in_specs=placed,
        out_specs=(P(("dp", "space"), None), P("dp", None), P()),
        check_vma=False,
    )
```

```python
import functools

import jax
import jax.numpy as jnp
from jax import lax
from jax.experimental import pallas as pl
from jax.experimental.pallas import tpu as pltpu
from jax.sharding import PartitionSpec as P

F32 = jnp.float32
BF16 = jnp.bfloat16
MESH = pl.DeviceIdType.MESH
NT = (((1,), (1,)), ((), ()))


def dot(a, b):
    return jnp.dot(a, b, preferred_element_type=F32)


def dot_nt(a, b):
    return lax.dot_general(a, b, NT, preferred_element_type=F32)


def body(n_dp, n_space, comm, feats, teacher, weight, nbrs, counts,
         to_x, to_w, out_loss,
         out_x, out_w,
         win, nbr_v, count_v, teach_v, w_v, w_t, hot, g_t, gw, part, rc, s0, r1, s1, r2, s2,
         rz, ag, gsend, grecv, lsum, lrecv,
         greeted, lsem, halo_s, halo_r, core_s, core_r, ring_s, ring_r, z_s, z_r, ag_s, ag_r, gh_s, gh_r, loss_s, loss_r):
    sites, chans = feats.shape
    outs = teacher.shape[1]
    offsets = nbrs.shape[0]
    edge = sites // 4
    slots = sites + 2 * edge
    nz = n_dp // 4
    z4 = nz // 4
    rows = offsets * chans // n_dp

    dp, sp = lax.axis_index("dp"), lax.axis_index("space")
    core = dp % 2
    z = (dp // 2) % nz
    xh = dp // (2 * nz)
    xl, y = sp // 4, sp % 4
    x = 2 * xh + xl

    def x_peer(step):
        to = (x + step) % 4
        return (dp + (to // 2 - xh) * 2 * nz, (to % 2) * 4 + y)

    def y_peer(step):
        return (dp, xl * 4 + (y + step) % 4)

    core_peer = (dp + 1 - 2 * core, sp)

    def z_peer(zz):
        return (xh * 2 * nz + zz * 2 + core, sp)

    def sp_peer(step):
        return (dp, (sp + step) % n_space)

    def remote(src, dst, send, recv, device):
        return pltpu.make_async_remote_copy(
            src_ref=src, dst_ref=dst, send_sem=send, recv_sem=recv, device_id=device, device_id_type=MESH)

    sent = []

    def start(copy):
        if comm:
            copy.start()
            sent.append(copy)

    def got(copy):
        if comm:
            copy.wait_recv()

    own_in = pltpu.make_async_copy(feats, win.at[pl.ds(edge, sites)], lsem.at[0])
    nbr_in = pltpu.make_async_copy(nbrs, nbr_v, lsem.at[1])
    w_in = pltpu.make_async_copy(weight, w_v, lsem.at[2])
    t_in = pltpu.make_async_copy(teacher, teach_v, lsem.at[3])
    nbr_in.start()
    own_in.start()
    w_in.start()
    t_in.start()
    c_in = pltpu.make_async_copy(counts, count_v, lsem.at[4])
    c_in.start()
    if comm:
        barrier = pltpu.get_barrier_semaphore()
        partners = [sp_peer(1), sp_peer(n_space - 1), z_peer((z + 1) % nz), z_peer((z + nz - 1) % nz)]
        partners += [x_peer(i) for i in (1, 3, 2)] + [y_peer(i) for i in (1, 3, 2)] + [core_peer]
        for device in partners:
            pl.semaphore_signal(barrier, inc=1, device_id=device, device_id_type=MESH)
        pl.semaphore_wait(barrier, len(partners))

    def greet(i):
        if comm and 2 ** i < nz // 2:
            for step in (2 ** i, nz - 2 ** i):
                pl.semaphore_signal(greeted.at[i], inc=1, device_id=z_peer((z + step) % nz), device_id_type=MESH)

    def greetings(i):
        if comm and 2 ** i < nz // 2:
            pl.semaphore_wait(greeted.at[i], 2)
            greet(i + 1)

    halo_up = remote(feats.at[pl.ds(sites - edge, edge)], win.at[pl.ds(0, edge)], halo_s.at[0], halo_r.at[0], sp_peer(1))
    halo_dn = remote(feats.at[pl.ds(0, edge)], win.at[pl.ds(edge + sites, edge)], halo_s.at[1], halo_r.at[1],
                     sp_peer(n_space - 1))
    start(halo_up)
    start(halo_dn)
    greet(0)

    nbr_in.wait()
    nbr_t = nbr_v[...]
    slot = lax.broadcasted_iota(jnp.int32, (slots, sites), 0)
    for k in range(offsets):
        hot[k] = (slot == nbr_t[k:k + 1, :]).astype(F32).astype(BF16)

    eye = (lax.broadcasted_iota(jnp.int32, (outs, outs), 0) == lax.broadcasted_iota(jnp.int32, (outs, outs), 1))
    eye = eye.astype(F32).astype(BF16)
    w_in.wait()
    for k in range(offsets):
        w_t[:, k * chans:(k + 1) * chans] = dot_nt(eye, w_v[k * chans:(k + 1) * chans, :]).astype(BF16)
    t_in.wait()
    teach_t = dot_nt(eye, teach_v[...])

    c_in.wait()
    count = count_v[...]
    flat = lax.broadcasted_iota(jnp.int32, count.shape, 0) * count.shape[1] + lax.broadcasted_iota(
        jnp.int32, count.shape, 1)
    limit = jnp.sum(jnp.where(flat == dp * n_space + sp, count, 0))
    total_count = jnp.sum(count)

    own_in.wait()
    got(halo_up)
    got(halo_dn)
    win_t = dot_nt(eye[:chans, :chans], win[...]).astype(BF16)
    for k in range(offsets):
        g_t[k * chans:(k + 1) * chans, :] = dot(win_t, hot[k]).astype(BF16)
    greetings(0)
    z_t = dot(w_t[...], g_t[...])
    at = lax.broadcasted_iota(jnp.int32, (outs, sites), 1)
    diff = jnp.where((at < limit - edge) | (at >= sites - edge), z_t - teach_t, F32(0.0))
    dz_t = (diff / outs).astype(BF16)
    square = jnp.sum((diff * diff).reshape(outs // 8, 8, sites), axis=0)
    lsum[0] = square[:, :128] + square[:, 128:]

    chain = [core_peer, x_peer(1 - 2 * (x % 2)), x_peer(2), y_peer(1 - 2 * (y % 2)), y_peer(2)]
    hop = 1
    while hop < nz:
        chain.append(z_peer(z + hop - 2 * hop * ((z // hop) % 2)))
        hop *= 2
    loss_copies = [remote(lsum.at[i], lrecv.at[i], loss_s.at[i], loss_r.at[i], chain[i]) for i in range(len(chain))]

    def loss_step(i):
        got(loss_copies[i])
        lsum[i + 1] = lsum[i] + lrecv[i]
        if i + 1 < len(chain):
            start(loss_copies[i + 1])

    start(loss_copies[0])

    core_copies = [remote(part.at[1 - core, s], rc.at[s], core_s.at[s], core_r.at[s], core_peer) for s in range(4)]

    def ring(s, level):
        return (x, x_peer) if (s < 2) == (level == 0) else (y, y_peer)

    steps = (1, 3, 2)
    ring_copies = [[[remote((s0, s1)[level].at[s, (ring(s, level)[0] + t) % 4], (r1, r2)[level].at[s, t],
                            ring_s.at[level, s, t], ring_r.at[level, s, t], ring(s, level)[1](t))
                     for t in steps] for s in range(4)] for level in range(2)]

    def after_core(s):
        got(core_copies[s])

        @pl.loop(0, 4)
        def _(i):
            s0[s, i] = (part[core, s, i].astype(F32) + rc[s, i].astype(F32)).astype(BF16)
        for copy in ring_copies[0][s]:
            start(copy)

    def after_x(s):
        for copy in ring_copies[0][s]:
            got(copy)
        mine = ring(s, 0)[0]
        for i in range(4):
            add = [s0[s, mine, i]] + [r1[s, t, i] for t in steps]
            s1[s, i] = sum(v.astype(F32) for v in add).astype(BF16)
        for copy in ring_copies[1][s]:
            start(copy)

    def after_y(s):
        for copy in ring_copies[1][s]:
            got(copy)
        add = [s1[s, ring(s, 1)[0]]] + [r2[s, t] for t in steps]
        s2[s] = sum(v.astype(F32) for v in add).astype(BF16)
        if comm:
            for j in range(z4):
                to = s * z4 + j
                back = (to - z + nz) % nz

                @pl.when(back != 0)
                def _():
                    remote(s2.at[s, j], rz.at[back], z_s.at[back], z_r.at[back], z_peer(to)).start()

    block = 2 * z4 * rows
    gw[:, block:, :] = jnp.zeros((2, gw.shape[1] - block, outs), F32)
    before = None
    for s in (0, 2, 1, 3):
        for h in range(2):
            base = (h * 4 + s) * block
            gw[h, :block, :] = dot_nt(g_t[base:base + block, :], dz_t)
            for j in range(z4):
                for c in range(2):
                    frame = gw[h, (j * 2 + c) * rows:(j * 2 + c) * rows + 64, :].astype(BF16)
                    for l in range(2):
                        for q in range(4):
                            at = (2 * h + l, q) if s < 2 else (q, 2 * h + l)
                            part[c, s, at[0], at[1], j] = frame[16 * q:16 * q + 16, 128 * l:128 * l + 128]
        start(core_copies[s])
        if before is not None:
            after_core(before)
        before = s
        if s == 1:
            loss_step(0)
            greetings(1)
    after_core(before)
    loss_step(1)
    greetings(2)

    def spread_part(first, last, acc):
        for k in range(first, last):
            d_t = dot(w_v[k * chans:(k + 1) * chans, :], dz_t).astype(BF16)
            acc = acc + dot_nt(d_t, hot[k])
        return acc

    spread = spread_part(0, offsets, jnp.zeros((chans, slots), F32))
    own = jnp.transpose(spread)
    gsend[0] = own[:edge].astype(BF16)
    gsend[1] = own[edge + sites:].astype(BF16)
    gh_dn = remote(gsend.at[0], grecv.at[0], gh_s.at[0], gh_r.at[0], sp_peer(n_space - 1))
    gh_up = remote(gsend.at[1], grecv.at[1], gh_s.at[1], gh_r.at[1], sp_peer(1))
    start(gh_dn)
    start(gh_up)
    loss_step(2)

    for s in (0, 2, 1, 3):
        after_x(s)
    loss_step(3)

    got(gh_dn)
    got(gh_up)
    out_x[edge:sites - edge, :] = own[2 * edge:sites].astype(BF16)
    out_x[:edge, :] = (own[edge:2 * edge] + grecv[1].astype(F32)).astype(BF16)
    out_x[sites - edge:, :] = (own[sites:sites + edge] + grecv[0].astype(F32)).astype(BF16)

    x_out = pltpu.make_async_copy(out_x, to_x, lsem.at[5])
    x_out.start()

    loss_step(4)
    for s in (0, 2, 1, 3):
        after_y(s)
    loss_step(5)
    loss_step(6)
    loss_step(7)

    total = s2[z // z4, z % z4].astype(F32)
    if comm:
        for t in range(1, nz):
            incoming = remote(rz.at[t], rz.at[t], z_s.at[t], z_r.at[t], z_peer(z))
            incoming.wait_recv()
            total = total + rz[t].astype(F32)
    ag[sp] = total
    ag_copies = []
    for u in range(1, n_space):
        copy = remote(ag.at[sp], ag.at[sp], ag_s.at[u], ag_r.at[u], sp_peer(u))
        start(copy)
    loss_step(8)
    loss_total = jnp.sum(lsum[len(chain)])
    out_loss[0, 0] = 0.5 * loss_total / (outs * total_count.astype(F32))
    if comm:
        for u in range(1, n_space):
            source = (sp - u + n_space) % n_space
            remote(ag.at[source], ag.at[source], ag_s.at[u], ag_r.at[u], sp_peer(u)).wait_recv()
    for p in range(8):
        q, h = p % 4, p // 4
        keep = min(16, rows - 16 * q)
        out_w[16 * q:16 * q + keep, 128 * h:128 * h + 128] = ag[p][:keep]
    w_out = pltpu.make_async_copy(out_w, to_w, lsem.at[6])
    w_out.start()
    for copy in sent:
        copy.wait_send()
    if comm:
        for t in range(1, nz):
            remote(rz.at[t], rz.at[t], z_s.at[t], z_r.at[t], z_peer(z)).wait_send()
    x_out.wait()
    w_out.wait()


def finish(x_in, w_in, x_out, w_out, x_v, w_v, sem):
    first = [pltpu.make_async_copy(x_in, x_v, sem.at[0]), pltpu.make_async_copy(w_in, w_v, sem.at[1])]
    second = [pltpu.make_async_copy(x_v, x_out, sem.at[2]), pltpu.make_async_copy(w_v, w_out, sem.at[3])]
    for copy in first:
        copy.start()
    for copy, then in zip(first, second):
        copy.wait()
        then.start()
    for copy in second:
        copy.wait()


def shards(n_dp, n_space, comm, features, teacher, weight, neighbours, counts):
    sites, chans = features.shape
    outs = teacher.shape[1]
    offsets = neighbours.shape[1]
    edge = sites // 4
    slots = sites + 2 * edge
    nz = n_dp // 4
    z4 = nz // 4
    rows = offsets * chans // n_dp
    assert 48 < rows <= 64 and n_space == 8 and outs == 256 and chans == 128
    n_loss = 5 + (nz - 1).bit_length()
    tile = (16, 128)
    dma = pltpu.SemaphoreType.DMA
    results = (
        jax.ShapeDtypeStruct((sites, chans), BF16),
        jax.ShapeDtypeStruct((rows, outs), F32),
        jax.ShapeDtypeStruct((1, 1), F32),
    )
    done = pl.pallas_call(
        functools.partial(body, n_dp, n_space, comm),
        out_shape=results,
        in_specs=[pl.BlockSpec(memory_space=pl.ANY)] * 5,
        out_specs=(
            pl.BlockSpec(memory_space=pl.ANY),
            pl.BlockSpec(memory_space=pl.ANY),
            pl.BlockSpec(memory_space=pltpu.SMEM),
        ),
        scratch_shapes=[
            pltpu.VMEM((sites, chans), BF16),
            pltpu.VMEM((rows, outs), F32),
            pltpu.VMEM((slots, chans), BF16),
            pltpu.VMEM((offsets, sites), jnp.int32),
            pltpu.VMEM((n_dp * n_space // 128, 128), jnp.int32),
            pltpu.VMEM((sites, outs), BF16),
            pltpu.VMEM((offsets * chans, outs), BF16),
            pltpu.VMEM((outs, offsets * chans), BF16),
            pltpu.VMEM((offsets, slots, sites), BF16),
            pltpu.VMEM((offsets * chans, sites), BF16),
            pltpu.VMEM((2, 2 * z4 * rows + 16, outs), F32),
            pltpu.VMEM((2, 4, 4, 4, z4) + tile, BF16),
            pltpu.VMEM((4, 4, 4, z4) + tile, BF16),
            pltpu.VMEM((4, 4, 4, z4) + tile, BF16),
            pltpu.VMEM((4, 4, 4, z4) + tile, BF16),
            pltpu.VMEM((4, 4, z4) + tile, BF16),
            pltpu.VMEM((4, 4, z4) + tile, BF16),
            pltpu.VMEM((4, z4) + tile, BF16),
            pltpu.VMEM((nz,) + tile, BF16),
            pltpu.VMEM((8,) + tile, F32),
            pltpu.VMEM((2, edge, chans), BF16),
            pltpu.VMEM((2, edge, chans), BF16),
            pltpu.VMEM((n_loss + 1, 8, 128), F32),
            pltpu.VMEM((n_loss, 8, 128), F32),
            pltpu.SemaphoreType.REGULAR((3,)),
            dma((7,)), dma((2,)), dma((2,)), dma((4,)), dma((4,)), dma((2, 4, 4)), dma((2, 4, 4)),
            dma((nz,)), dma((nz,)), dma((n_space,)), dma((n_space,)), dma((2,)), dma((2,)),
            dma((n_loss,)), dma((n_loss,)),
        ],
        compiler_params=pltpu.CompilerParams(
            vmem_limit_bytes=56 * 1024 * 1024,
            **(dict(collective_id=0, has_side_effects=True) if comm else {})),
    )(features, teacher, weight, neighbours.T, counts.reshape(-1, 128))
    anywhere = [pl.BlockSpec(memory_space=pl.ANY)] * 2
    grad_x, grad_w = pl.pallas_call(
        finish, out_shape=results[:2], in_specs=anywhere, out_specs=tuple(anywhere),
        scratch_shapes=[pltpu.VMEM((sites, chans), BF16), pltpu.VMEM((rows, outs), F32), dma((4,))],
        compiler_params=pltpu.CompilerParams(vmem_limit_bytes=56 * 1024 * 1024),
    )(*done[:2])
    return grad_x, grad_w, done[2].reshape(())


def solution(mesh, comm=True):
    placed = (
        P(("dp", "space"), None),
        P(("dp", "space"), None),
        P(),
        P(("dp", "space"), None),
        P(),
    )
    return jax.shard_map(
        functools.partial(shards, mesh.shape["dp"], mesh.shape["space"], comm),
        mesh=mesh,
        in_specs=placed,
        out_specs=(P(("dp", "space"), None), P("dp", None), P()),
        check_vma=False,
    )
```

```python
import functools

import jax
import jax.numpy as jnp
from jax import lax
from jax.experimental import pallas as pl
from jax.experimental.pallas import tpu as pltpu
from jax.sharding import PartitionSpec as P

F32 = jnp.float32
BF16 = jnp.bfloat16
MESH = pl.DeviceIdType.MESH
NT = (((1,), (1,)), ((), ()))


def dot(a, b):
    return jnp.dot(a, b, preferred_element_type=F32)


def dot_nt(a, b):
    return lax.dot_general(a, b, NT, preferred_element_type=F32)


def body(n_dp, n_space, comm, feats, teacher, weight, nbrs, counts,
         to_x, to_w, out_loss,
         out_x, out_w,
         win, nbr_v, count_v, teach_v, w_v, w_t, hot, g_t, gw, part, rc, s0, r1, s1, r2, s2,
         rz, ag, gsend, grecv, lsum, lrecv,
         greeted, lsem, halo_s, halo_r, core_s, core_r, ring_s, ring_r, z_s, z_r, ag_s, ag_r, gh_s, gh_r, loss_s, loss_r):
    sites, chans = feats.shape
    outs = teacher.shape[1]
    offsets = nbrs.shape[0]
    edge = sites // 4
    slots = sites + 2 * edge
    nz = n_dp // 4
    z4 = nz // 4
    rows = offsets * chans // n_dp

    dp, sp = lax.axis_index("dp"), lax.axis_index("space")
    core = dp % 2
    z = (dp // 2) % nz
    xh = dp // (2 * nz)
    xl, y = sp // 4, sp % 4
    x = 2 * xh + xl

    def x_peer(step):
        to = (x + step) % 4
        return (dp + (to // 2 - xh) * 2 * nz, (to % 2) * 4 + y)

    def y_peer(step):
        return (dp, xl * 4 + (y + step) % 4)

    core_peer = (dp + 1 - 2 * core, sp)

    def z_peer(zz):
        return (xh * 2 * nz + zz * 2 + core, sp)

    def sp_peer(step):
        return (dp, (sp + step) % n_space)

    def remote(src, dst, send, recv, device):
        return pltpu.make_async_remote_copy(
            src_ref=src, dst_ref=dst, send_sem=send, recv_sem=recv, device_id=device, device_id_type=MESH)

    sent = []

    def start(copy):
        if comm:
            copy.start()
            sent.append(copy)

    def got(copy):
        if comm:
            copy.wait_recv()

    own_in = pltpu.make_async_copy(feats, win.at[pl.ds(0, sites)], lsem.at[0])
    nbr_in = pltpu.make_async_copy(nbrs, nbr_v, lsem.at[1])
    w_in = pltpu.make_async_copy(weight, w_v, lsem.at[2])
    t_in = pltpu.make_async_copy(teacher, teach_v, lsem.at[3])
    if comm:
        barrier = pltpu.get_barrier_semaphore()
        partners = [sp_peer(1), sp_peer(n_space - 1), z_peer((z + 1) % nz), z_peer((z + nz - 1) % nz)]
        partners += [x_peer(i) for i in (1, 3, 2)] + [y_peer(i) for i in (1, 3, 2)] + [core_peer]
        for device in partners:
            pl.semaphore_signal(barrier, inc=1, device_id=device, device_id_type=MESH)
    own_in.start()
    nbr_in.start()
    w_in.start()
    t_in.start()
    c_in = pltpu.make_async_copy(counts, count_v, lsem.at[4])
    c_in.start()
    own_in.wait()
    if comm:
        pl.semaphore_wait(barrier, len(partners))

    def greet(i):
        if comm and 2 ** i < nz // 2:
            for step in (2 ** i, nz - 2 ** i):
                pl.semaphore_signal(greeted.at[i], inc=1, device_id=z_peer((z + step) % nz), device_id_type=MESH)

    def greetings(i):
        if comm and 2 ** i < nz // 2:
            pl.semaphore_wait(greeted.at[i], 2)
            greet(i + 1)

    halo_up = remote(win.at[pl.ds(sites - edge, edge)], win.at[pl.ds(sites, edge)], halo_s.at[0], halo_r.at[0], sp_peer(1))
    halo_dn = remote(win.at[pl.ds(0, edge)], win.at[pl.ds(sites + edge, edge)], halo_s.at[1], halo_r.at[1],
                     sp_peer(n_space - 1))
    start(halo_up)
    start(halo_dn)
    greet(0)

    nbr_in.wait()
    nbr_t = nbr_v[...]
    nbr_t = jnp.where((nbr_t >= edge) & (nbr_t < edge + sites), nbr_t - edge,
                      jnp.where((nbr_t >= 0) & (nbr_t < edge), nbr_t + sites, nbr_t))
    slot = lax.broadcasted_iota(jnp.int32, (slots, sites), 0)
    for k in range(offsets):
        hot[k] = (slot == nbr_t[k:k + 1, :]).astype(F32).astype(BF16)

    eye = (lax.broadcasted_iota(jnp.int32, (outs, outs), 0) == lax.broadcasted_iota(jnp.int32, (outs, outs), 1))
    eye = eye.astype(F32).astype(BF16)
    w_in.wait()
    for k in range(offsets):
        w_t[:, k * chans:(k + 1) * chans] = dot_nt(eye, w_v[k * chans:(k + 1) * chans, :]).astype(BF16)
    t_in.wait()
    teach_t = dot_nt(eye, teach_v[...])

    c_in.wait()
    count = count_v[...]
    flat = lax.broadcasted_iota(jnp.int32, count.shape, 0) * count.shape[1] + lax.broadcasted_iota(
        jnp.int32, count.shape, 1)
    limit = jnp.sum(jnp.where(flat == dp * n_space + sp, count, 0))
    total_count = jnp.sum(count)

    own_t = dot_nt(eye[:chans, :chans], win[:sites, :]).astype(BF16)
    for k in range(offsets):
        g_t[k * chans:(k + 1) * chans, :] = dot(own_t, hot[k, :sites, :]).astype(BF16)
    got(halo_up)
    got(halo_dn)
    edge_t = dot_nt(eye[:chans, :chans], win[sites:, :]).astype(BF16)
    for k in range(offsets):
        at = slice(k * chans, (k + 1) * chans)
        g_t[at, :] = (g_t[at, :].astype(F32) + dot(edge_t, hot[k, sites:, :])).astype(BF16)
    greetings(0)
    z_t = dot(w_t[...], g_t[...])
    at = lax.broadcasted_iota(jnp.int32, (outs, sites), 1)
    diff = jnp.where((at < limit - edge) | (at >= sites - edge), z_t - teach_t, F32(0.0))
    dz_t = (diff / outs).astype(BF16)
    square = jnp.sum((diff * diff).reshape(outs // 8, 8, sites), axis=0)
    lsum[0] = square[:, :128] + square[:, 128:]

    def loss_stage(stage, place, size, device, base):
        come = lrecv.at[pl.ds(base, size)]

        def copy(t, source):
            return remote(lsum.at[stage], come.at[source], loss_s.at[base + t], loss_r.at[base + t], device(t))

        def send():
            come[place] = lsum[stage]
            for t in range(1, size):
                start(copy(t, place))

        def collect():
            for t in range(1, size):
                got(copy(t, (place - t + size) % size))
            lsum[stage + 1] = sum(come[i] for i in range(1, size)) + come[0]

        return send, collect

    stages = [
        loss_stage(0, z, nz, lambda t: z_peer((z + t) % nz), 0),
        loss_stage(1, x, 4, x_peer, nz),
        loss_stage(2, y, 4, y_peer, nz + 4),
        loss_stage(3, core, 2, lambda t: core_peer, nz + 8),
    ]

    core_copies = [remote(part.at[1 - core, s], rc.at[s], core_s.at[s], core_r.at[s], core_peer) for s in range(4)]

    def ring(s, level):
        return (x, x_peer) if (s < 2) == (level == 0) else (y, y_peer)

    steps = (1, 3, 2)
    ring_copies = [[[remote((s0, s1)[level].at[s, (ring(s, level)[0] + t) % 4], (r1, r2)[level].at[s, t],
                            ring_s.at[level, s, t], ring_r.at[level, s, t], ring(s, level)[1](t))
                     for t in steps] for s in range(4)] for level in range(2)]

    def after_core(s):
        got(core_copies[s])

        @pl.loop(0, 4)
        def _(i):
            s0[s, i] = (part[core, s, i].astype(F32) + rc[s, i].astype(F32)).astype(BF16)
        for copy in ring_copies[0][s]:
            start(copy)

    def after_x(s):
        for copy in ring_copies[0][s]:
            got(copy)
        mine = ring(s, 0)[0]
        for i in range(4):
            add = [s0[s, mine, i]] + [r1[s, t, i] for t in steps]
            s1[s, i] = sum(v.astype(F32) for v in add).astype(BF16)
        for copy in ring_copies[1][s]:
            start(copy)

    def after_y(ahead):
        s = (z // z4 + ahead) % 4
        for t in steps:
            if comm:
                remote(r2.at[s, t], r2.at[s, t], ring_s.at[1, s, t], ring_r.at[1, s, t], core_peer).wait_recv()
        first = s // 2
        add = [s1[s, y + first * (x - y)]] + [r2[s, t] for t in steps]
        s2[s] = sum(v.astype(F32) for v in add).astype(BF16)
        if comm:
            for j in range(z4):
                to = s * z4 + j
                back = (to - z + nz) % nz

                @pl.when(back != 0)
                def _():
                    remote(s2.at[s, j], rz.at[back], z_s.at[back], z_r.at[back], z_peer(to)).start()

    block = 2 * z4 * rows
    gw[:, block:, :] = jnp.zeros((2, gw.shape[1] - block, outs), F32)
    before = None
    for s in (0, 2, 1, 3):
        for h in range(2):
            base = (h * 4 + s) * block
            gw[h, :block, :] = dot_nt(g_t[base:base + block, :], dz_t)
            for j in range(z4):
                for c in range(2):
                    frame = gw[h, (j * 2 + c) * rows:(j * 2 + c) * rows + 64, :].astype(BF16)
                    for l in range(2):
                        for q in range(4):
                            at = (2 * h + l, q) if s < 2 else (q, 2 * h + l)
                            part[c, s, at[0], at[1], j] = frame[16 * q:16 * q + 16, 128 * l:128 * l + 128]
        start(core_copies[s])
        if before is not None:
            after_core(before)
        before = s
        if s == 1:
            greetings(1)
    after_core(before)
    greetings(2)
    stages[0][0]()

    def spread_part(first, last, acc):
        for k in range(first, last):
            d_t = dot(w_v[k * chans:(k + 1) * chans, :], dz_t).astype(BF16)
            acc = acc + dot_nt(d_t, hot[k])
        return acc

    spread = spread_part(0, offsets, jnp.zeros((chans, slots), F32))
    own = jnp.transpose(spread)
    gsend[0] = own[sites:sites + edge].astype(BF16)
    gsend[1] = own[sites + edge:].astype(BF16)
    gh_dn = remote(gsend.at[0], grecv.at[0], gh_s.at[0], gh_r.at[0], sp_peer(n_space - 1))
    gh_up = remote(gsend.at[1], grecv.at[1], gh_s.at[1], gh_r.at[1], sp_peer(1))
    start(gh_dn)
    start(gh_up)

    for s in (0, 2, 1, 3):
        after_x(s)
    stages[0][1]()
    stages[1][0]()

    got(gh_dn)
    got(gh_up)
    out_x[edge:sites - edge, :] = own[edge:sites - edge].astype(BF16)
    out_x[:edge, :] = (own[:edge] + grecv[1].astype(F32)).astype(BF16)
    out_x[sites - edge:, :] = (own[sites - edge:sites] + grecv[0].astype(F32)).astype(BF16)
    x_out = pltpu.make_async_copy(out_x, to_x, lsem.at[5])
    x_out.start()

    for ahead in (2, 1, 3, 0):
        after_y(ahead)
    stages[1][1]()
    stages[2][0]()

    total = s2[z // z4, z % z4].astype(F32)
    if comm:
        for t in range(1, nz):
            incoming = remote(rz.at[t], rz.at[t], z_s.at[t], z_r.at[t], z_peer(z))
            incoming.wait_recv()
            total = total + rz[t].astype(F32)
    ag[sp] = total
    ag_copies = []
    for u in range(1, n_space):
        copy = remote(ag.at[sp], ag.at[sp], ag_s.at[u], ag_r.at[u], sp_peer(u))
        start(copy)
    stages[2][1]()
    stages[3][0]()
    stages[3][1]()
    loss_total = jnp.sum(lsum[4])
    out_loss[0, 0] = 0.5 * loss_total / (outs * total_count.astype(F32))
    if comm:
        for u in range(1, n_space):
            source = (sp - u + n_space) % n_space
            remote(ag.at[source], ag.at[source], ag_s.at[u], ag_r.at[u], sp_peer(u)).wait_recv()
    for p in range(8):
        q, h = p % 4, p // 4
        keep = min(16, rows - 16 * q)
        out_w[16 * q:16 * q + keep, 128 * h:128 * h + 128] = ag[p][:keep]
    w_out = pltpu.make_async_copy(out_w, to_w, lsem.at[6])
    w_out.start()
    for copy in sent:
        copy.wait_send()
    if comm:
        for t in range(1, nz):
            remote(rz.at[t], rz.at[t], z_s.at[t], z_r.at[t], z_peer(z)).wait_send()
    x_out.wait()
    w_out.wait()


def finish(x_in, w_in, l_in, x_out, w_out, l_out, x_v, w_v, sem):
    l_out[0, 0] = l_in[0, 0]
    first = [pltpu.make_async_copy(x_in, x_v, sem.at[0]), pltpu.make_async_copy(w_in, w_v, sem.at[1])]
    second = [pltpu.make_async_copy(x_v, x_out, sem.at[2]), pltpu.make_async_copy(w_v, w_out, sem.at[3])]
    for copy in first:
        copy.start()
    for copy, then in zip(first, second):
        copy.wait()
        then.start()
    for copy in second:
        copy.wait()


def shards(n_dp, n_space, comm, features, teacher, weight, neighbours, counts):
    sites, chans = features.shape
    outs = teacher.shape[1]
    offsets = neighbours.shape[1]
    edge = sites // 4
    slots = sites + 2 * edge
    nz = n_dp // 4
    z4 = nz // 4
    rows = offsets * chans // n_dp
    assert 48 < rows <= 64 and n_space == 8 and outs == 256 and chans == 128
    n_loss = nz + 10
    tile = (16, 128)
    dma = pltpu.SemaphoreType.DMA
    results = (
        jax.ShapeDtypeStruct((sites, chans), BF16),
        jax.ShapeDtypeStruct((rows, outs), F32),
        jax.ShapeDtypeStruct((1, 1), F32),
    )
    done = pl.pallas_call(
        functools.partial(body, n_dp, n_space, comm),
        out_shape=results,
        in_specs=[pl.BlockSpec(memory_space=pl.ANY)] * 5,
        out_specs=(
            pl.BlockSpec(memory_space=pl.ANY),
            pl.BlockSpec(memory_space=pl.ANY),
            pl.BlockSpec(memory_space=pltpu.SMEM),
        ),
        scratch_shapes=[
            pltpu.VMEM((sites, chans), BF16),
            pltpu.VMEM((rows, outs), F32),
            pltpu.VMEM((slots, chans), BF16),
            pltpu.VMEM((offsets, sites), jnp.int32),
            pltpu.VMEM((n_dp * n_space // 128, 128), jnp.int32),
            pltpu.VMEM((sites, outs), BF16),
            pltpu.VMEM((offsets * chans, outs), BF16),
            pltpu.VMEM((outs, offsets * chans), BF16),
            pltpu.VMEM((offsets, slots, sites), BF16),
            pltpu.VMEM((offsets * chans, sites), BF16),
            pltpu.VMEM((2, 2 * z4 * rows + 16, outs), F32),
            pltpu.VMEM((2, 4, 4, 4, z4) + tile, BF16),
            pltpu.VMEM((4, 4, 4, z4) + tile, BF16),
            pltpu.VMEM((4, 4, 4, z4) + tile, BF16),
            pltpu.VMEM((4, 4, 4, z4) + tile, BF16),
            pltpu.VMEM((4, 4, z4) + tile, BF16),
            pltpu.VMEM((4, 4, z4) + tile, BF16),
            pltpu.VMEM((4, z4) + tile, BF16),
            pltpu.VMEM((nz,) + tile, BF16),
            pltpu.VMEM((8,) + tile, F32),
            pltpu.VMEM((2, edge, chans), BF16),
            pltpu.VMEM((2, edge, chans), BF16),
            pltpu.VMEM((5, 8, 128), F32),
            pltpu.VMEM((n_loss, 8, 128), F32),
            pltpu.SemaphoreType.REGULAR((3,)),
            dma((7,)), dma((2,)), dma((2,)), dma((4,)), dma((4,)), dma((2, 4, 4)), dma((2, 4, 4)),
            dma((nz,)), dma((nz,)), dma((n_space,)), dma((n_space,)), dma((2,)), dma((2,)),
            dma((n_loss,)), dma((n_loss,)),
        ],
        compiler_params=pltpu.CompilerParams(
            vmem_limit_bytes=56 * 1024 * 1024,
            **(dict(collective_id=0, has_side_effects=True) if comm else {})),
    )(features, teacher, weight, neighbours.T, counts.reshape(-1, 128))
    anywhere = [pl.BlockSpec(memory_space=pl.ANY)] * 2
    scalar = [pl.BlockSpec(memory_space=pltpu.SMEM)]
    grad_x, grad_w, loss = pl.pallas_call(
        finish, out_shape=results, in_specs=anywhere + scalar, out_specs=tuple(anywhere + scalar),
        scratch_shapes=[pltpu.VMEM((sites, chans), BF16), pltpu.VMEM((rows, outs), F32), dma((4,))],
        compiler_params=pltpu.CompilerParams(vmem_limit_bytes=56 * 1024 * 1024),
    )(*done)
    return grad_x, grad_w, loss.reshape(())


def solution(mesh, comm=True):
    placed = (
        P(("dp", "space"), None),
        P(("dp", "space"), None),
        P(),
        P(("dp", "space"), None),
        P(),
    )
    return jax.shard_map(
        functools.partial(shards, mesh.shape["dp"], mesh.shape["space"], comm),
        mesh=mesh,
        in_specs=placed,
        out_specs=(P(("dp", "space"), None), P("dp", None), P()),
        check_vma=False,
    )
```

```python
import functools

import jax
import jax.numpy as jnp
from jax import lax
from jax.experimental import pallas as pl
from jax.experimental.pallas import tpu as pltpu
from jax.sharding import PartitionSpec as P

F32 = jnp.float32
BF16 = jnp.bfloat16
MESH = pl.DeviceIdType.MESH
NT = (((1,), (1,)), ((), ()))


def dot(a, b):
    return jnp.dot(a, b, preferred_element_type=F32)


def dot_nt(a, b):
    return lax.dot_general(a, b, NT, preferred_element_type=F32)


def body(n_dp, n_space, comm, feats, teacher, weight, nbrs, counts,
         to_x, ag, to_loss,
         out_x, out_w, out_loss,
         win, nbr_v, count_v, teach_v, w_v, w_t, hot, hot_edge, g_t, gw, part, rc, s0, r1, s1, r2, s2,
         rz, gsend, grecv, lsum, lrecv,
         greeted, lsem, halo_s, halo_r, core_s, core_r, ring_s, ring_r, z_s, z_r, ag_s, ag_r, gh_s, gh_r, loss_s, loss_r):
    sites, chans = feats.shape
    outs = teacher.shape[1]
    offsets = nbrs.shape[0]
    edge = sites // 4
    slots = sites + 2 * edge
    nz = n_dp // 4
    z4 = nz // 4
    rows = offsets * chans // n_dp

    dp, sp = lax.axis_index("dp"), lax.axis_index("space")
    core = dp % 2
    z = (dp // 2) % nz
    xh = dp // (2 * nz)
    xl, y = sp // 4, sp % 4
    x = 2 * xh + xl

    def x_peer(step):
        to = (x + step) % 4
        return (dp + (to // 2 - xh) * 2 * nz, (to % 2) * 4 + y)

    def y_peer(step):
        return (dp, xl * 4 + (y + step) % 4)

    core_peer = (dp + 1 - 2 * core, sp)

    def z_peer(zz):
        return (xh * 2 * nz + zz * 2 + core, sp)

    def sp_peer(step):
        return (dp, (sp + step) % n_space)

    def remote(src, dst, send, recv, device):
        return pltpu.make_async_remote_copy(
            src_ref=src, dst_ref=dst, send_sem=send, recv_sem=recv, device_id=device, device_id_type=MESH)

    sent = []

    def start(copy):
        if comm:
            copy.start()
            sent.append(copy)

    def got(copy):
        if comm:
            copy.wait_recv()

    own_in = pltpu.make_async_copy(feats, win.at[pl.ds(0, sites)], lsem.at[0])
    nbr_in = pltpu.make_async_copy(nbrs, nbr_v, lsem.at[1])
    w_in = pltpu.make_async_copy(weight, w_v, lsem.at[2])
    t_in = pltpu.make_async_copy(teacher, teach_v, lsem.at[3])
    if comm:
        barrier = pltpu.get_barrier_semaphore()
        partners = [sp_peer(1), sp_peer(n_space - 1), z_peer((z + 1) % nz), z_peer((z + nz - 1) % nz)]
        partners += [x_peer(i) for i in (1, 3, 2)] + [y_peer(i) for i in (1, 3, 2)] + [core_peer]
        for device in partners:
            pl.semaphore_signal(barrier, inc=1, device_id=device, device_id_type=MESH)
    own_in.start()
    nbr_in.start()
    w_in.start()
    t_in.start()
    c_in = pltpu.make_async_copy(counts, count_v, lsem.at[4])
    c_in.start()
    own_in.wait()
    if comm:
        pl.semaphore_wait(barrier, len(partners))

    def greet(i):
        if comm and 2 ** i < nz // 2:
            for step in (2 ** i, nz - 2 ** i):
                pl.semaphore_signal(greeted.at[i], inc=1, device_id=z_peer((z + step) % nz), device_id_type=MESH)

    def greetings(i):
        if comm and 2 ** i < nz // 2:
            pl.semaphore_wait(greeted.at[i], 2)
            greet(i + 1)

    halo_up = remote(win.at[pl.ds(sites - edge, edge)], win.at[pl.ds(sites, edge)], halo_s.at[0], halo_r.at[0], sp_peer(1))
    halo_dn = remote(win.at[pl.ds(0, edge)], win.at[pl.ds(sites + edge, edge)], halo_s.at[1], halo_r.at[1],
                     sp_peer(n_space - 1))
    start(halo_up)
    start(halo_dn)
    greet(0)

    nbr_in.wait()
    nbr_t = nbr_v[...]
    nbr_t = jnp.where((nbr_t >= edge) & (nbr_t < edge + sites), nbr_t - edge,
                      jnp.where((nbr_t >= 0) & (nbr_t < edge), nbr_t + sites, nbr_t))
    slot = lax.broadcasted_iota(jnp.int32, (slots, sites), 0)
    for k in range(offsets):
        one = (slot == nbr_t[k:k + 1, :]).astype(F32).astype(BF16)
        hot[k] = one[:sites]
        hot_edge[k] = one[sites:]

    eye = (lax.broadcasted_iota(jnp.int32, (outs, outs), 0) == lax.broadcasted_iota(jnp.int32, (outs, outs), 1))
    eye = eye.astype(F32).astype(BF16)
    w_in.wait()
    for k in range(offsets):
        w_t[:, k * chans:(k + 1) * chans] = dot_nt(eye, w_v[k * chans:(k + 1) * chans, :]).astype(BF16)
    t_in.wait()
    teach_t = dot_nt(eye, teach_v[...])

    c_in.wait()
    count = count_v[...]
    flat = lax.broadcasted_iota(jnp.int32, count.shape, 0) * count.shape[1] + lax.broadcasted_iota(
        jnp.int32, count.shape, 1)
    limit = jnp.sum(jnp.where(flat == dp * n_space + sp, count, 0))
    total_count = jnp.sum(count)

    own_t = dot_nt(eye[:chans, :chans], win[:sites, :]).astype(BF16)
    for k in range(offsets):
        g_t[k * chans:(k + 1) * chans, :] = dot(own_t, hot[k]).astype(BF16)
    got(halo_up)
    got(halo_dn)
    edge_t = dot_nt(eye[:chans, :chans], win[sites:, :]).astype(BF16)
    blank = jnp.zeros((chans, 2 * edge), BF16)
    edge_2 = jnp.concatenate([jnp.concatenate([edge_t, blank], axis=1), jnp.concatenate([blank, edge_t], axis=1)], axis=0)
    for k in range(0, offsets, 2):
        n = min(2, offsets - k)
        at = slice(k * chans, (k + n) * chans)
        pair = hot_edge[k:k + n].reshape(n * 2 * edge, sites)
        g_t[at, :] = (g_t[at, :].astype(F32) + dot(edge_2[:n * chans, :n * 2 * edge], pair)).astype(BF16)
    greetings(0)
    z_t = dot(w_t[...], g_t[...])
    at = lax.broadcasted_iota(jnp.int32, (outs, sites), 1)
    diff = jnp.where((at < limit - edge) | (at >= sites - edge), z_t - teach_t, F32(0.0))
    dz_t = (diff / outs).astype(BF16)
    square = jnp.sum((diff * diff).reshape(outs // 8, 8, sites), axis=0)
    lsum[0] = square[:, :128] + square[:, 128:]

    def loss_stage(stage, place, size, device, base):
        come = lrecv.at[pl.ds(base, size)]

        def copy(t, source):
            return remote(lsum.at[stage], come.at[source], loss_s.at[base + t], loss_r.at[base + t], device(t))

        def send():
            come[place] = lsum[stage]
            for t in range(1, size):
                start(copy(t, place))

        def collect():
            for t in range(1, size):
                got(copy(t, (place - t + size) % size))
            lsum[stage + 1] = sum(come[i] for i in range(1, size)) + come[0]

        return send, collect

    stages = [
        loss_stage(0, z, nz, lambda t: z_peer((z + t) % nz), 0),
        loss_stage(1, x, 4, x_peer, nz),
        loss_stage(2, y, 4, y_peer, nz + 4),
        loss_stage(3, core, 2, lambda t: core_peer, nz + 8),
    ]

    core_copies = [remote(part.at[1 - core, s], rc.at[s], core_s.at[s], core_r.at[s], core_peer) for s in range(4)]

    def ring(s, level):
        return (x, x_peer) if (s < 2) == (level == 0) else (y, y_peer)

    steps = (2, 1, 3)
    ring_copies = [[[remote((s0, s1)[level].at[s, (ring(s, level)[0] + t) % 4], (r1, r2)[level].at[s, t],
                            ring_s.at[level, s, t], ring_r.at[level, s, t], ring(s, level)[1](t))
                     for t in steps] for s in range(4)] for level in range(2)]

    def after_core(s):
        got(core_copies[s])

        @pl.loop(0, 4)
        def _(i):
            s0[s, i] = (part[core, s, i].astype(F32) + rc[s, i].astype(F32)).astype(BF16)
        for copy in ring_copies[0][s]:
            start(copy)

    def after_x(s):
        for copy in ring_copies[0][s]:
            got(copy)
        mine = ring(s, 0)[0]
        for i in range(4):
            add = [s0[s, mine, i]] + [r1[s, t, i] for t in steps]
            s1[s, i] = sum(v.astype(F32) for v in add).astype(BF16)
        for copy in ring_copies[1][s]:
            start(copy)

    def after_y(ahead):
        s = (z // z4 + ahead) % 4
        for t in steps:
            if comm:
                remote(r2.at[s, t], r2.at[s, t], ring_s.at[1, s, t], ring_r.at[1, s, t], core_peer).wait_recv()
        first = s // 2
        add = [s1[s, y + first * (x - y)]] + [r2[s, t] for t in steps]
        s2[s] = sum(v.astype(F32) for v in add).astype(BF16)
        if comm:
            for j in range(z4):
                to = s * z4 + j
                back = (to - z + nz) % nz

                @pl.when(back != 0)
                def _():
                    remote(s2.at[s, j], rz.at[back], z_s.at[back], z_r.at[back], z_peer(to)).start()

    block = 2 * z4 * rows
    gw[:, block:, :] = jnp.zeros((8, gw.shape[1] - block, outs), F32)
    order = [(s, h) for s in (0, 2, 1, 3) for h in range(2)]

    def product(s, h):
        base = (h * 4 + s) * block
        gw[h * 4 + s, :block, :] = dot_nt(g_t[base:base + block, :], dz_t)

    product(*order[0])
    before = None
    for i, (s, h) in enumerate(order):
        if i + 1 < len(order):
            product(*order[i + 1])
        for j in range(z4):
            for c in range(2):
                frame = gw[h * 4 + s, (j * 2 + c) * rows:(j * 2 + c) * rows + 64, :].astype(BF16)
                for l in range(2):
                    for q in range(4):
                        at = (2 * h + l, q) if s < 2 else (q, 2 * h + l)
                        part[c, s, at[0], at[1], j] = frame[16 * q:16 * q + 16, 128 * l:128 * l + 128]
        if h == 1:
            start(core_copies[s])
            if before is not None:
                after_core(before)
            before = s
            if s == 1:
                greetings(1)
    after_core(before)
    greetings(2)
    stages[0][0]()

    spread = jnp.zeros((chans, sites), F32)
    spread_edge = jnp.zeros((chans, 2 * edge), F32)
    for k in range(offsets):
        d_t = dot(w_v[k * chans:(k + 1) * chans, :], dz_t).astype(BF16)
        spread = spread + dot_nt(d_t, hot[k])
        spread_edge = spread_edge + dot_nt(d_t, hot_edge[k])
    own = jnp.transpose(spread)
    away = jnp.transpose(spread_edge)
    gsend[0] = away[:edge].astype(BF16)
    gsend[1] = away[edge:].astype(BF16)
    gh_dn = remote(gsend.at[0], grecv.at[0], gh_s.at[0], gh_r.at[0], sp_peer(n_space - 1))
    gh_up = remote(gsend.at[1], grecv.at[1], gh_s.at[1], gh_r.at[1], sp_peer(1))
    start(gh_dn)
    start(gh_up)

    for s in (0, 2, 1, 3):
        after_x(s)
    stages[0][1]()
    stages[1][0]()

    got(gh_dn)
    got(gh_up)
    out_x[edge:sites - edge, :] = own[edge:sites - edge].astype(BF16)
    out_x[:edge, :] = (own[:edge] + grecv[1].astype(F32)).astype(BF16)
    out_x[sites - edge:, :] = (own[sites - edge:sites] + grecv[0].astype(F32)).astype(BF16)
    x_out = pltpu.make_async_copy(out_x, to_x, lsem.at[5])
    x_out.start()

    for ahead in (2, 1, 3, 0):
        after_y(ahead)
    stages[1][1]()
    stages[2][0]()

    total = s2[z // z4, z % z4].astype(F32)
    if comm:
        for t in range(1, nz):
            incoming = remote(rz.at[t], rz.at[t], z_s.at[t], z_r.at[t], z_peer(z))
            incoming.wait_recv()
            total = total + rz[t].astype(F32)
    out_w[...] = total
    w_out = pltpu.make_async_copy(out_w, ag.at[sp], lsem.at[6])
    w_out.start()
    for u in (6, 2, 3, 5, 4, 1, 7):
        start(remote(out_w, ag.at[sp], ag_s.at[u], ag_r.at[u], sp_peer(u)))
    stages[2][1]()
    stages[3][0]()
    stages[3][1]()
    loss_total = jnp.sum(lsum[4], keepdims=True)
    out_loss[...] = 0.5 * loss_total / (outs * total_count.astype(F32))
    l_out = pltpu.make_async_copy(out_loss, to_loss, lsem.at[7])
    l_out.start()
    if comm:
        for u in range(1, n_space):
            source = (sp - u + n_space) % n_space
            remote(out_w, ag.at[source], ag_s.at[u], ag_r.at[u], sp_peer(u)).wait_recv()
    for copy in sent:
        copy.wait_send()
    if comm:
        for t in range(1, nz):
            remote(rz.at[t], rz.at[t], z_s.at[t], z_r.at[t], z_peer(z)).wait_send()
    x_out.wait()
    w_out.wait()
    l_out.wait()


def finish(x_in, pieces_in, l_in, x_out, w_out, l_out, x_v, pieces, w_v, l_v, sem):
    first = [pltpu.make_async_copy(a, b, sem.at[i])
             for i, (a, b) in enumerate(((x_in, x_v), (l_in, l_v), (pieces_in, pieces)))]
    second = [pltpu.make_async_copy(a, b, sem.at[3 + i])
              for i, (a, b) in enumerate(((x_v, x_out), (l_v, l_out), (w_v, w_out)))]
    for copy in first:
        copy.start()
    for i in range(2):
        first[i].wait()
        second[i].start()
    first[2].wait()
    for p in range(8):
        q, h = p % 4, p // 4
        keep = min(16, w_v.shape[0] - 16 * q)
        w_v[16 * q:16 * q + keep, 128 * h:128 * h + 128] = pieces[p][:keep]
    second[2].start()
    for copy in second:
        copy.wait()


def shards(n_dp, n_space, comm, features, teacher, weight, neighbours, counts):
    sites, chans = features.shape
    outs = teacher.shape[1]
    offsets = neighbours.shape[1]
    edge = sites // 4
    slots = sites + 2 * edge
    nz = n_dp // 4
    z4 = nz // 4
    rows = offsets * chans // n_dp
    assert 48 < rows <= 64 and n_space == 8 and outs == 256 and chans == 128
    n_loss = nz + 10
    tile = (16, 128)
    dma = pltpu.SemaphoreType.DMA
    results = (
        jax.ShapeDtypeStruct((sites, chans), BF16),
        jax.ShapeDtypeStruct((rows, outs), F32),
        jax.ShapeDtypeStruct((1, 1), F32),
    )
    done = pl.pallas_call(
        functools.partial(body, n_dp, n_space, comm),
        out_shape=(results[0], jax.ShapeDtypeStruct((8,) + tile, F32), results[2]),
        in_specs=[pl.BlockSpec(memory_space=pl.ANY)] * 5,
        out_specs=(
            pl.BlockSpec(memory_space=pl.ANY),
            pl.BlockSpec(memory_space=pl.ANY),
            pl.BlockSpec(memory_space=pl.ANY),
        ),
        scratch_shapes=[
            pltpu.VMEM((sites, chans), BF16),
            pltpu.VMEM(tile, F32),
            pltpu.VMEM((1, 1), F32),
            pltpu.VMEM((slots, chans), BF16),
            pltpu.VMEM((offsets, sites), jnp.int32),
            pltpu.VMEM((n_dp * n_space // 128, 128), jnp.int32),
            pltpu.VMEM((sites, outs), BF16),
            pltpu.VMEM((offsets * chans, outs), BF16),
            pltpu.VMEM((outs, offsets * chans), BF16),
            pltpu.VMEM((offsets, sites, sites), BF16),
            pltpu.VMEM((offsets, 2 * edge, sites), BF16),
            pltpu.VMEM((offsets * chans, sites), BF16),
            pltpu.VMEM((8, 2 * z4 * rows + 16, outs), F32),
            pltpu.VMEM((2, 4, 4, 4, z4) + tile, BF16),
            pltpu.VMEM((4, 4, 4, z4) + tile, BF16),
            pltpu.VMEM((4, 4, 4, z4) + tile, BF16),
            pltpu.VMEM((4, 4, 4, z4) + tile, BF16),
            pltpu.VMEM((4, 4, z4) + tile, BF16),
            pltpu.VMEM((4, 4, z4) + tile, BF16),
            pltpu.VMEM((4, z4) + tile, BF16),
            pltpu.VMEM((nz,) + tile, BF16),
            pltpu.VMEM((2, edge, chans), BF16),
            pltpu.VMEM((2, edge, chans), BF16),
            pltpu.VMEM((5, 8, 128), F32),
            pltpu.VMEM((n_loss, 8, 128), F32),
            pltpu.SemaphoreType.REGULAR((3,)),
            dma((8,)), dma((2,)), dma((2,)), dma((4,)), dma((4,)), dma((2, 4, 4)), dma((2, 4, 4)),
            dma((nz,)), dma((nz,)), dma((n_space,)), dma((n_space,)), dma((2,)), dma((2,)),
            dma((n_loss,)), dma((n_loss,)),
        ],
        compiler_params=pltpu.CompilerParams(
            vmem_limit_bytes=56 * 1024 * 1024,
            **(dict(collective_id=0, has_side_effects=True) if comm else {})),
    )(features, teacher, weight, neighbours.T, counts.reshape(-1, 128))
    anywhere = [pl.BlockSpec(memory_space=pl.ANY)] * 3
    grad_x, grad_w, loss = pl.pallas_call(
        finish, out_shape=results, in_specs=anywhere, out_specs=tuple(anywhere),
        scratch_shapes=[pltpu.VMEM((sites, chans), BF16), pltpu.VMEM((8,) + tile, F32), pltpu.VMEM((rows, outs), F32),
                        pltpu.VMEM((1, 1), F32), dma((6,))],
        compiler_params=pltpu.CompilerParams(vmem_limit_bytes=56 * 1024 * 1024),
    )(*done)
    return grad_x, grad_w, loss.reshape(())


def solution(mesh, comm=True):
    placed = (
        P(("dp", "space"), None),
        P(("dp", "space"), None),
        P(),
        P(("dp", "space"), None),
        P(),
    )
    return jax.shard_map(
        functools.partial(shards, mesh.shape["dp"], mesh.shape["space"], comm),
        mesh=mesh,
        in_specs=placed,
        out_specs=(P(("dp", "space"), None), P("dp", None), P()),
        check_vma=False,
    )
```

```python
import functools

import jax
import jax.numpy as jnp
from jax import lax
from jax.experimental import pallas as pl
from jax.experimental.pallas import tpu as pltpu
from jax.sharding import PartitionSpec as P

F32 = jnp.float32
BF16 = jnp.bfloat16
MESH = pl.DeviceIdType.MESH
NT = (((1,), (1,)), ((), ()))


def dot(a, b):
    return jnp.dot(a, b, preferred_element_type=F32)


def dot_nt(a, b):
    return lax.dot_general(a, b, NT, preferred_element_type=F32)


def body(n_dp, n_space, comm, feats, teacher, weight, nbrs, counts,
         to_x, ag, to_loss,
         out_x, out_w, out_loss,
         win, nbr_v, count_v, teach_v, w_v, w_t, hot, hot_edge, g_t, gw, part, rc, s0, r1, s1, r2, s2,
         rz, gsend, grecv, lsum, lrecv,
         greeted, lsem, halo_s, halo_r, core_s, core_r, ring_s, ring_r, z_s, z_r, ag_s, ag_r, gh_s, gh_r, loss_s, loss_r):
    sites, chans = feats.shape
    outs = teacher.shape[1]
    offsets = nbrs.shape[0]
    edge = sites // 4
    slots = sites + 2 * edge
    nz = n_dp // 4
    z4 = nz // 4
    rows = offsets * chans // n_dp

    dp, sp = lax.axis_index("dp"), lax.axis_index("space")
    core = dp % 2
    z = (dp // 2) % nz
    xh = dp // (2 * nz)
    xl, y = sp // 4, sp % 4
    x = 2 * xh + xl

    def x_peer(step):
        to = (x + step) % 4
        return (dp + (to // 2 - xh) * 2 * nz, (to % 2) * 4 + y)

    def y_peer(step):
        return (dp, xl * 4 + (y + step) % 4)

    core_peer = (dp + 1 - 2 * core, sp)

    def z_peer(zz):
        return (xh * 2 * nz + zz * 2 + core, sp)

    def sp_peer(step):
        return (dp, (sp + step) % n_space)

    def remote(src, dst, send, recv, device):
        return pltpu.make_async_remote_copy(
            src_ref=src, dst_ref=dst, send_sem=send, recv_sem=recv, device_id=device, device_id_type=MESH)

    sent = []

    def start(copy):
        if comm:
            copy.start()
            sent.append(copy)

    def got(copy):
        if comm:
            copy.wait_recv()

    own_in = pltpu.make_async_copy(feats, win.at[pl.ds(0, sites)], lsem.at[0])
    nbr_in = pltpu.make_async_copy(nbrs, nbr_v, lsem.at[1])
    w_in = pltpu.make_async_copy(weight, w_v, lsem.at[2])
    t_in = pltpu.make_async_copy(teacher, teach_v, lsem.at[3])
    if comm:
        barrier = pltpu.get_barrier_semaphore()
        partners = [sp_peer(1), sp_peer(n_space - 1), z_peer((z + 1) % nz), z_peer((z + nz - 1) % nz)]
        partners += [x_peer(i) for i in (1, 3, 2)] + [y_peer(i) for i in (1, 3, 2)] + [core_peer]
        for device in partners:
            pl.semaphore_signal(barrier, inc=1, device_id=device, device_id_type=MESH)
    own_in.start()
    nbr_in.start()
    w_in.start()
    t_in.start()
    c_in = pltpu.make_async_copy(counts, count_v, lsem.at[4])
    c_in.start()
    own_in.wait()
    if comm:
        pl.semaphore_wait(barrier, len(partners))

    def greet(i):
        if comm and 2 ** i < nz // 2:
            for step in (2 ** i, nz - 2 ** i):
                pl.semaphore_signal(greeted.at[i], inc=1, device_id=z_peer((z + step) % nz), device_id_type=MESH)

    def greetings(i):
        if comm and 2 ** i < nz // 2:
            pl.semaphore_wait(greeted.at[i], 2)
            greet(i + 1)

    halo_up = remote(win.at[pl.ds(sites - edge, edge)], win.at[pl.ds(sites, edge)], halo_s.at[0], halo_r.at[0], sp_peer(1))
    halo_dn = remote(win.at[pl.ds(0, edge)], win.at[pl.ds(sites + edge, edge)], halo_s.at[1], halo_r.at[1],
                     sp_peer(n_space - 1))
    start(halo_up)
    start(halo_dn)
    greet(0)

    nbr_in.wait()
    nbr_t = nbr_v[...]
    nbr_t = jnp.where((nbr_t >= edge) & (nbr_t < edge + sites), nbr_t - edge,
                      jnp.where((nbr_t >= 0) & (nbr_t < edge), nbr_t + sites, nbr_t))
    slot = lax.broadcasted_iota(jnp.int32, (slots, sites), 0)
    for k in range(offsets):
        one = (slot == nbr_t[k:k + 1, :]).astype(F32).astype(BF16)
        hot[k] = one[:sites]
        hot_edge[k] = one[sites:]

    eye = (lax.broadcasted_iota(jnp.int32, (outs, outs), 0) == lax.broadcasted_iota(jnp.int32, (outs, outs), 1))
    eye = eye.astype(F32).astype(BF16)
    w_in.wait()
    for k in range(offsets):
        w_t[:, k * chans:(k + 1) * chans] = dot_nt(eye, w_v[k * chans:(k + 1) * chans, :]).astype(BF16)
    t_in.wait()
    teach_t = dot_nt(eye, teach_v[...])

    c_in.wait()
    count = count_v[...]
    flat = lax.broadcasted_iota(jnp.int32, count.shape, 0) * count.shape[1] + lax.broadcasted_iota(
        jnp.int32, count.shape, 1)
    limit = jnp.sum(jnp.where(flat == dp * n_space + sp, count, 0))
    total_count = jnp.sum(count)

    own_t = dot_nt(eye[:chans, :chans], win[:sites, :]).astype(BF16)
    for k in range(offsets):
        g_t[k * chans:(k + 1) * chans, :] = dot(own_t, hot[k]).astype(BF16)
    got(halo_up)
    got(halo_dn)
    edge_t = dot_nt(eye[:chans, :chans], win[sites:, :]).astype(BF16)
    blank = jnp.zeros((chans, 2 * edge), BF16)
    edge_2 = jnp.concatenate([jnp.concatenate([edge_t, blank], axis=1), jnp.concatenate([blank, edge_t], axis=1)], axis=0)
    for k in range(0, offsets, 2):
        n = min(2, offsets - k)
        at = slice(k * chans, (k + n) * chans)
        pair = hot_edge[k:k + n].reshape(n * 2 * edge, sites)
        g_t[at, :] = (g_t[at, :].astype(F32) + dot(edge_2[:n * chans, :n * 2 * edge], pair)).astype(BF16)
    greetings(0)
    z_t = dot(w_t[...], g_t[...])
    at = lax.broadcasted_iota(jnp.int32, (outs, sites), 1)
    diff = jnp.where((at < limit - edge) | (at >= sites - edge), z_t - teach_t, F32(0.0))
    dz_t = (diff / outs).astype(BF16)
    square = jnp.sum((diff * diff).reshape(outs // 8, 8, sites), axis=0)
    lsum[0] = square[:, :128] + square[:, 128:]

    def loss_stage(stage, place, size, device, base):
        come = lrecv.at[pl.ds(base, size)]

        def copy(t, source):
            return remote(lsum.at[stage], come.at[source], loss_s.at[base + t], loss_r.at[base + t], device(t))

        def send():
            come[place] = lsum[stage]
            for t in range(1, size):
                start(copy(t, place))

        def collect():
            for t in range(1, size):
                got(copy(t, (place - t + size) % size))
            lsum[stage + 1] = sum(come[i] for i in range(1, size)) + come[0]

        return send, collect

    stages = [
        loss_stage(0, z, nz, lambda t: z_peer((z + t) % nz), 0),
        loss_stage(1, x, 4, x_peer, nz),
        loss_stage(2, y, 4, y_peer, nz + 4),
        loss_stage(3, core, 2, lambda t: core_peer, nz + 8),
    ]

    core_copies = [remote(part.at[1 - core, s], rc.at[s], core_s.at[s], core_r.at[s], core_peer) for s in range(4)]

    def ring(s, level):
        return (x, x_peer) if (s < 2) == (level == 0) else (y, y_peer)

    steps = (2, 1, 3)
    ring_copies = [[[remote((s0, s1)[level].at[s, (ring(s, level)[0] + t) % 4], (r1, r2)[level].at[s, t],
                            ring_s.at[level, s, t], ring_r.at[level, s, t], ring(s, level)[1](t))
                     for t in steps] for s in range(4)] for level in range(2)]

    def after_core(s):
        got(core_copies[s])

        @pl.loop(0, 4)
        def _(i):
            s0[s, i] = (part[core, s, i].astype(F32) + rc[s, i].astype(F32)).astype(BF16)
        for copy in ring_copies[0][s]:
            start(copy)

    def after_x(s):
        for copy in ring_copies[0][s]:
            got(copy)
        mine = ring(s, 0)[0]
        for i in range(4):
            add = [s0[s, mine, i]] + [r1[s, t, i] for t in steps]
            s1[s, i] = sum(v.astype(F32) for v in add).astype(BF16)
        for copy in ring_copies[1][s]:
            start(copy)

    def after_y(ahead):
        s = (z // z4 + ahead) % 4
        for t in steps:
            if comm:
                remote(r2.at[s, t], r2.at[s, t], ring_s.at[1, s, t], ring_r.at[1, s, t], core_peer).wait_recv()
        first = s // 2
        add = [s1[s, y + first * (x - y)]] + [r2[s, t] for t in steps]
        s2[s] = sum(v.astype(F32) for v in add).astype(BF16)
        if comm:
            for j in range(z4):
                to = s * z4 + j
                back = (to - z + nz) % nz

                @pl.when(back != 0)
                def _():
                    remote(s2.at[s, j], rz.at[back], z_s.at[back], z_r.at[back], z_peer(to)).start()

    block = 2 * z4 * rows
    gw[:, block:, :] = jnp.zeros((8, gw.shape[1] - block, outs), F32)
    order = [(s, h) for s in (0, 2, 1, 3) for h in range(2)]

    def product(s, h):
        base = (h * 4 + s) * block
        gw[h * 4 + s, :block, :] = dot_nt(g_t[base:base + block, :], dz_t)

    product(*order[0])
    before = None
    for i, (s, h) in enumerate(order):
        if i + 1 < len(order):
            product(*order[i + 1])
        for j in range(z4):
            for c in range(2):
                frame = gw[h * 4 + s, (j * 2 + c) * rows:(j * 2 + c) * rows + 64, :].astype(BF16)
                for l in range(2):
                    for q in range(4):
                        at = (2 * h + l, q) if s < 2 else (q, 2 * h + l)
                        part[c, s, at[0], at[1], j] = frame[16 * q:16 * q + 16, 128 * l:128 * l + 128]
        if h == 1:
            start(core_copies[s])
            if before is not None:
                after_core(before)
            before = s
            if s == 1:
                greetings(1)
    after_core(before)
    greetings(2)
    stages[0][0]()

    g_t[...] = dot(w_v[...], dz_t).astype(BF16)
    spread = jnp.zeros((chans, sites), F32)
    spread_edge = jnp.zeros((chans, 2 * edge), F32)
    for k in range(offsets):
        d_t = g_t[k * chans:(k + 1) * chans, :]
        spread = spread + dot_nt(d_t, hot[k])
        spread_edge = spread_edge + dot_nt(d_t, hot_edge[k])
    own = jnp.transpose(spread)
    away = jnp.transpose(spread_edge)
    gsend[0] = away[:edge].astype(BF16)
    gsend[1] = away[edge:].astype(BF16)
    gh_dn = remote(gsend.at[0], grecv.at[0], gh_s.at[0], gh_r.at[0], sp_peer(n_space - 1))
    gh_up = remote(gsend.at[1], grecv.at[1], gh_s.at[1], gh_r.at[1], sp_peer(1))
    start(gh_dn)
    start(gh_up)

    for s in (0, 2, 1, 3):
        after_x(s)
    stages[0][1]()
    stages[1][0]()

    got(gh_dn)
    got(gh_up)
    out_x[edge:sites - edge, :] = own[edge:sites - edge].astype(BF16)
    out_x[:edge, :] = (own[:edge] + grecv[1].astype(F32)).astype(BF16)
    out_x[sites - edge:, :] = (own[sites - edge:sites] + grecv[0].astype(F32)).astype(BF16)
    x_out = pltpu.make_async_copy(out_x, to_x, lsem.at[5])
    x_out.start()

    for ahead in (2, 1, 3, 0):
        after_y(ahead)
    stages[1][1]()
    stages[2][0]()

    total = s2[z // z4, z % z4].astype(F32)
    if comm:
        for t in range(1, nz):
            incoming = remote(rz.at[t], rz.at[t], z_s.at[t], z_r.at[t], z_peer(z))
            incoming.wait_recv()
            total = total + rz[t].astype(F32)
    out_w[...] = total
    w_out = pltpu.make_async_copy(out_w, ag.at[sp], lsem.at[6])
    w_out.start()
    for u in (6, 2, 3, 5, 4, 1, 7):
        start(remote(out_w, ag.at[sp], ag_s.at[u], ag_r.at[u], sp_peer(u)))
    stages[2][1]()
    stages[3][0]()
    stages[3][1]()
    loss_total = jnp.sum(lsum[4], keepdims=True)
    out_loss[...] = 0.5 * loss_total / (outs * total_count.astype(F32))
    l_out = pltpu.make_async_copy(out_loss, to_loss, lsem.at[7])
    l_out.start()
    if comm:
        for u in range(1, n_space):
            source = (sp - u + n_space) % n_space
            remote(out_w, ag.at[source], ag_s.at[u], ag_r.at[u], sp_peer(u)).wait_recv()
    for copy in sent:
        copy.wait_send()
    if comm:
        for t in range(1, nz):
            remote(rz.at[t], rz.at[t], z_s.at[t], z_r.at[t], z_peer(z)).wait_send()
    x_out.wait()
    w_out.wait()
    l_out.wait()


def finish(x_in, pieces_in, l_in, x_out, w_out, l_out, x_v, pieces, w_v, l_v, sem):
    first = [pltpu.make_async_copy(a, b, sem.at[i])
             for i, (a, b) in enumerate(((x_in, x_v), (l_in, l_v), (pieces_in, pieces)))]
    second = [pltpu.make_async_copy(a, b, sem.at[3 + i])
              for i, (a, b) in enumerate(((x_v, x_out), (l_v, l_out), (w_v, w_out)))]
    for copy in first:
        copy.start()
    for i in range(2):
        first[i].wait()
        second[i].start()
    first[2].wait()
    for p in range(8):
        q, h = p % 4, p // 4
        keep = min(16, w_v.shape[0] - 16 * q)
        w_v[16 * q:16 * q + keep, 128 * h:128 * h + 128] = pieces[p][:keep]
    second[2].start()
    for copy in second:
        copy.wait()


def shards(n_dp, n_space, comm, features, teacher, weight, neighbours, counts):
    sites, chans = features.shape
    outs = teacher.shape[1]
    offsets = neighbours.shape[1]
    edge = sites // 4
    slots = sites + 2 * edge
    nz = n_dp // 4
    z4 = nz // 4
    rows = offsets * chans // n_dp
    assert 48 < rows <= 64 and n_space == 8 and outs == 256 and chans == 128
    n_loss = nz + 10
    tile = (16, 128)
    dma = pltpu.SemaphoreType.DMA
    results = (
        jax.ShapeDtypeStruct((sites, chans), BF16),
        jax.ShapeDtypeStruct((rows, outs), F32),
        jax.ShapeDtypeStruct((1, 1), F32),
    )
    done = pl.pallas_call(
        functools.partial(body, n_dp, n_space, comm),
        out_shape=(results[0], jax.ShapeDtypeStruct((8,) + tile, F32), results[2]),
        in_specs=[pl.BlockSpec(memory_space=pl.ANY)] * 5,
        out_specs=(
            pl.BlockSpec(memory_space=pl.ANY),
            pl.BlockSpec(memory_space=pl.ANY),
            pl.BlockSpec(memory_space=pl.ANY),
        ),
        scratch_shapes=[
            pltpu.VMEM((sites, chans), BF16),
            pltpu.VMEM(tile, F32),
            pltpu.VMEM((1, 1), F32),
            pltpu.VMEM((slots, chans), BF16),
            pltpu.VMEM((offsets, sites), jnp.int32),
            pltpu.VMEM((n_dp * n_space // 128, 128), jnp.int32),
            pltpu.VMEM((sites, outs), BF16),
            pltpu.VMEM((offsets * chans, outs), BF16),
            pltpu.VMEM((outs, offsets * chans), BF16),
            pltpu.VMEM((offsets, sites, sites), BF16),
            pltpu.VMEM((offsets, 2 * edge, sites), BF16),
            pltpu.VMEM((offsets * chans, sites), BF16),
            pltpu.VMEM((8, 2 * z4 * rows + 16, outs), F32),
            pltpu.VMEM((2, 4, 4, 4, z4) + tile, BF16),
            pltpu.VMEM((4, 4, 4, z4) + tile, BF16),
            pltpu.VMEM((4, 4, 4, z4) + tile, BF16),
            pltpu.VMEM((4, 4, 4, z4) + tile, BF16),
            pltpu.VMEM((4, 4, z4) + tile, BF16),
            pltpu.VMEM((4, 4, z4) + tile, BF16),
            pltpu.VMEM((4, z4) + tile, BF16),
            pltpu.VMEM((nz,) + tile, BF16),
            pltpu.VMEM((2, edge, chans), BF16),
            pltpu.VMEM((2, edge, chans), BF16),
            pltpu.VMEM((5, 8, 128), F32),
            pltpu.VMEM((n_loss, 8, 128), F32),
            pltpu.SemaphoreType.REGULAR((3,)),
            dma((8,)), dma((2,)), dma((2,)), dma((4,)), dma((4,)), dma((2, 4, 4)), dma((2, 4, 4)),
            dma((nz,)), dma((nz,)), dma((n_space,)), dma((n_space,)), dma((2,)), dma((2,)),
            dma((n_loss,)), dma((n_loss,)),
        ],
        compiler_params=pltpu.CompilerParams(
            vmem_limit_bytes=56 * 1024 * 1024,
            **(dict(collective_id=0, has_side_effects=True) if comm else {})),
    )(features, teacher, weight, neighbours.T, counts.reshape(-1, 128))
    anywhere = [pl.BlockSpec(memory_space=pl.ANY)] * 3
    grad_x, grad_w, loss = pl.pallas_call(
        finish, out_shape=results, in_specs=anywhere, out_specs=tuple(anywhere),
        scratch_shapes=[pltpu.VMEM((sites, chans), BF16), pltpu.VMEM((8,) + tile, F32), pltpu.VMEM((rows, outs), F32),
                        pltpu.VMEM((1, 1), F32), dma((6,))],
        compiler_params=pltpu.CompilerParams(vmem_limit_bytes=56 * 1024 * 1024),
    )(*done)
    return grad_x, grad_w, loss.reshape(())


def solution(mesh, comm=True):
    placed = (
        P(("dp", "space"), None),
        P(("dp", "space"), None),
        P(),
        P(("dp", "space"), None),
        P(),
    )
    return jax.shard_map(
        functools.partial(shards, mesh.shape["dp"], mesh.shape["space"], comm),
        mesh=mesh,
        in_specs=placed,
        out_specs=(P(("dp", "space"), None), P("dp", None), P()),
        check_vma=False,
    )
```
